512 devices in a mesh: sub: 32 (over z_lo, x, core), reg: 16 (over z_hi, y).
Axes of the slice: x: 4, y: 4, z: 16 (z_hi: 4, z_lo: 4; z = z_hi * 4 + z_lo), core: 2. Of those that a mesh axis runs over, the one named last changes fastest.
Arguments:
- right_side: float32 [32, 16, 1280, 16], P('sub', 'reg'), may hold values from -6 to 6
- tiles: bfloat16 [32, 16, 80, 128, 128], P('sub', 'reg'), may hold values from -1 to 5
- tile_list: int32 [32, 16, 80, 2], P('sub', 'reg'), may hold values from 0 to 9, as said below
- weights: float32 [32, 16, 1280], P('sub', 'reg'), may hold values from 0.15 to 0.35
- face_map: int32 [32, 16, 6], P('sub', 'reg'), may hold values from 0 to 9, as said below
- matching: int32 [32, 16, 6, 128], P('sub', 'reg'), may hold values from 0 to 127, each once within a row
- coarse_basis: bfloat16 [32, 16, 1280, 128], P('sub', 'reg'), may hold values from -0.15625 to 0.15625
- coarse_map: int32 [32, 16, 128], P('sub', 'reg'), may hold values from 0 to 2047, as said below
- coarse_inverse: float32 [16, 2048, 2048], P('reg', 'sub'), may hold values from -1 to 2, as said below
Outputs:
- solution: bfloat16 [32, 16, 1280, 16], P('sub', 'reg')
- residual: bfloat16 [32, 16, 1280, 16], P('sub', 'reg')
The draws below stay inside these ranges and needn't reach their ends.
Inputs may be any that keep to these rules, and one draw needn't show every extreme that they name: `tile_list`: entries 0 to 9 of each subdomain's list are (b, b) for b in order; the other 70 entries are distinct off-diagonal block pairs. `face_map`: the six blocks of a subdomain are distinct. `coarse_map`: A subdomain's 128 numbers are distinct, and within a subregion every number is named by exactly two subdomains. `coarse_inverse`: symmetric in its last two dimensions.
All inputs are finite; a program needn't handle non-finite values.
Results may differ from the reference program's by a relative error of at most 0.0075.
Values may be sent and summed in bfloat16 or wider, within the bound.
A program may use at most 64 MiB of HBM per device.

```python
import math
import jax
import jax.numpy as jnp
from jax import lax

ORDER = 1280
TILE = 128
RIGHTS = 16
COARSE = 128
SWEEPS = 3
BLOCKS = 10
LISTED = 80
SUBS = 32
REGIONS = 16
COARSE_ALL = 2048
N_REG = 16


def draw_tiles(key, part):
    keys = jax.random.split(key, SUBS * REGIONS)
    spread = 0.6 / math.sqrt(ORDER)

    def single(device_key):
        first, second = jax.random.split(device_key)
        entries = jnp.clip(jax.random.normal(first, (LISTED, TILE, TILE), jnp.float32), -4.0, 4.0)
        entries = entries * spread
        diagonal = jnp.exp(jax.random.uniform(second, (BLOCKS, TILE), jnp.float32, math.log(2.0), math.log(4.0)))
        identity = jnp.eye(TILE, dtype=jnp.float32)
        entries = entries.at[:BLOCKS].add(diagonal[:, :, None] * identity[None])
        return entries.astype(jnp.bfloat16)
    return lax.map(single, keys).reshape(SUBS, REGIONS, LISTED, TILE, TILE)


def draw_tile_list(key, part):
    keys = jax.random.split(key, SUBS * REGIONS)

    def single(device_key):
        order = jax.random.permutation(device_key, BLOCKS * (BLOCKS - 1))[:LISTED - BLOCKS].astype(jnp.int32)
        rows = order // (BLOCKS - 1)
        other = order % (BLOCKS - 1)
        columns = other + (other >= rows).astype(jnp.int32)
        diagonal = jnp.arange(BLOCKS, dtype=jnp.int32)
        return jnp.stack([jnp.concatenate([diagonal, rows]), jnp.concatenate([diagonal, columns])], axis=-1)
    return jax.vmap(single)(keys).reshape(SUBS, REGIONS, LISTED, 2)


def draw_face_map(key, part):
    keys = jax.random.split(key, SUBS * REGIONS)

    def single(device_key):
        return jax.random.permutation(device_key, BLOCKS)[:6].astype(jnp.int32)
    return jax.vmap(single)(keys).reshape(SUBS, REGIONS, 6)


def draw_coarse_map(key, part):
    keys = jax.random.split(key, REGIONS)
    half = COARSE // 2

    def single(region_key):
        label_key, order_key, shift_key, shuffle_key = jax.random.split(region_key, 4)
        labels = jax.random.permutation(label_key, COARSE_ALL).astype(jnp.int32).reshape(SUBS, half)
        placing = jax.random.permutation(order_key, SUBS).astype(jnp.int32)
        ranking = jnp.zeros((SUBS,), jnp.int32).at[placing].set(jnp.arange(SUBS, dtype=jnp.int32))
        shifts = jax.random.randint(shift_key, (half,), 1, SUBS).astype(jnp.int32)
        source_rank = (ranking[:, None] - shifts[None, :]) % SUBS
        source = placing[source_rank]
        columns = jnp.broadcast_to(jnp.arange(half, dtype=jnp.int32)[None, :], (SUBS, half))
        second = labels[source, columns]
        combined = jnp.concatenate([labels, second], axis=1)
        shuffle_keys = jax.random.split(shuffle_key, SUBS)
        orders = jax.vmap(lambda one_key: jax.random.permutation(one_key, COARSE).astype(jnp.int32))(shuffle_keys)
        return jnp.take_along_axis(combined, orders, axis=1)
    return jnp.transpose(jax.vmap(single)(keys), (1, 0, 2))


def draw_coarse_inverse(key, part):
    keys = jax.random.split(key, REGIONS)

    def single(region_key):
        first, second = jax.random.split(region_key)
        raw = jnp.clip(jax.random.normal(first, (COARSE_ALL, COARSE_ALL), jnp.float32), -4.0, 4.0)
        raw = raw * (0.3 / math.sqrt(COARSE_ALL))
        symmetric = (raw + raw.T) / math.sqrt(2.0)
        diagonal = jnp.exp(jax.random.uniform(second, (COARSE_ALL,), jnp.float32, math.log(0.5), math.log(1.5)))
        return symmetric + jnp.diag(diagonal)
    return lax.map(single, keys)


def block_scale(own_key, shape, cuts, least, top_value):
    loudness = 1.0
    for position, shards_of in cuts:
        draws = jax.random.uniform(jax.random.fold_in(jax.random.fold_in(own_key, 6), position), (shards_of,), jnp.float32, least / len(cuts), top_value / len(cuts))
        loudness = loudness * jnp.repeat(jnp.exp(draws), shape[position] // shards_of).reshape((-1,) + (1,) * (len(shape) - 1 - position))
    return loudness


def scatter_about(rng, dims, width, bound, shards=(), held_as=jnp.bfloat16):
    values = width * jax.random.normal(rng, dims, jnp.float32)
    if shards:
        values = values * block_scale(rng, dims, shards, -0.22, 0.18)
    return jnp.clip(values, -bound, bound).astype(held_as)


def setup_inputs(seed: int = 0) -> dict:
    seeds = jax.random.split(jax.random.key(seed), 10)
    return {
        "right_side": scatter_about(seeds[0], (SUBS, REGIONS, ORDER, RIGHTS), 1.0, 6.0, ((0, 32), (1, 16)), jnp.float32),
        "tiles": draw_tiles(jax.random.fold_in(seeds[9], 71), 0),
        "tile_list": draw_tile_list(jax.random.fold_in(seeds[9], 71), 0),
        "weights": jnp.clip(jnp.exp(math.log(0.35) - 0.8472978 * jax.random.uniform(seeds[3], (SUBS, REGIONS, ORDER), jnp.float32) ** block_scale(seeds[3], (SUBS, REGIONS, ORDER), ((0, 32), (1, 16)), -0.2, 0.2)), 0.15, 0.35),
        "face_map": draw_face_map(jax.random.fold_in(seeds[9], 71), 0),
        "matching": jax.vmap(lambda own: jax.random.permutation(own, TILE))(jax.random.split(seeds[5], SUBS * REGIONS * 6)).reshape((SUBS, REGIONS, 6, TILE)).astype(jnp.int32),
        "coarse_basis": scatter_about(seeds[6], (SUBS, REGIONS, ORDER, COARSE), ORDER ** -0.5, 0.15625, ((0, 32), (1, 16))),
        "coarse_map": draw_coarse_map(jax.random.fold_in(seeds[9], 71), 0),
        "coarse_inverse": draw_coarse_inverse(jax.random.fold_in(seeds[9], 71), 0),
    }


def subdomain_products(tiles, tile_list, values):
    total = SUBS * REGIONS
    flat_tiles = tiles.reshape(total, LISTED, TILE, TILE)
    flat_lists = tile_list.reshape(total, LISTED, 2)
    flat_values = values.reshape(total, ORDER, RIGHTS)

    def single(item):
        block, listing, vector = item
        low = lax.optimization_barrier(vector.astype(jnp.bfloat16)).astype(jnp.float32)
        low = low.reshape(BLOCKS, TILE, RIGHTS)
        picked = low[listing[:, 1]]
        products = jnp.einsum("tij,tjr->tir", block.astype(jnp.float32), picked, precision=lax.Precision.HIGHEST)
        table = (listing[:, 0][None, :] == jnp.arange(BLOCKS, dtype=jnp.int32)[:, None]).astype(jnp.float32)
        summed = jnp.einsum("bt,tir->bir", table, products, precision=lax.Precision.HIGHEST)
        return summed.reshape(ORDER, RIGHTS)

    return lax.map(single, (flat_tiles, flat_lists, flat_values)).reshape(SUBS, REGIONS, ORDER, RIGHTS)


def face_coupling(values, face_map, matching):
    stride = max(N_REG // 4, 1)
    stacked = values.reshape(SUBS, REGIONS, BLOCKS, TILE, RIGHTS)
    faces = jnp.take_along_axis(stacked, face_map[:, :, :, None, None], axis=2)
    moves = ((1, 1), (1, -1), (1, stride), (1, -stride), (0, 1), (0, -1))
    coupling = jnp.zeros_like(stacked)
    block_ids = jnp.arange(BLOCKS, dtype=jnp.int32)
    for face in range(6):
        along, offset = moves[face]
        arrived = jnp.roll(faces[:, :, face ^ 1], offset, axis=along)
        permuted = jnp.take_along_axis(arrived, matching[:, :, face, :, None], axis=2)
        table = (face_map[:, :, face][:, :, None] == block_ids[None, None, :]).astype(jnp.float32)
        coupling = coupling + table[:, :, :, None, None] * permuted[:, :, None]
    return coupling.reshape(SUBS, REGIONS, ORDER, RIGHTS)


def operator(values, tiles, tile_list, face_map, matching):
    return subdomain_products(tiles, tile_list, values) - 0.5 * face_coupling(values, face_map, matching)


def precondition(residual, weights, coarse_basis, coarse_map, coarse_inverse):
    basis = coarse_basis.astype(jnp.float32)
    low = lax.optimization_barrier(residual.astype(jnp.bfloat16)).astype(jnp.float32)
    local_coarse = jnp.einsum("sgmn,sgmr->sgnr", basis, low, precision=lax.Precision.HIGHEST)
    region_ids = jnp.broadcast_to(jnp.arange(REGIONS, dtype=jnp.int32)[None, :, None], (SUBS, REGIONS, COARSE))
    assembled = jnp.zeros((REGIONS, COARSE_ALL, RIGHTS), jnp.float32).at[region_ids, coarse_map].add(local_coarse)
    coarse_solution = jnp.einsum("gab,gbr->gar", coarse_inverse, assembled, precision=lax.Precision.HIGHEST)
    own = coarse_solution[region_ids, coarse_map]
    own_low = lax.optimization_barrier(own.astype(jnp.bfloat16)).astype(jnp.float32)
    correction = jnp.einsum("sgmn,sgnr->sgmr", basis, own_low, precision=lax.Precision.HIGHEST)
    return weights[:, :, :, None] * residual + correction


def reference(right_side, tiles, tile_list, weights, face_map, matching, coarse_basis, coarse_map, coarse_inverse):
    solution = jnp.zeros_like(right_side)
    residual = right_side
    for sweep in range(SWEEPS):
        solution = solution + precondition(residual, weights, coarse_basis, coarse_map, coarse_inverse)
        residual = right_side - operator(solution, tiles, tile_list, face_map, matching)
    return solution.astype(jnp.bfloat16), residual.astype(jnp.bfloat16)
```

```python
import functools

import jax
import jax.numpy as jnp
from jax import lax
from jax.experimental import pallas as pl
from jax.experimental.pallas import tpu as pltpu
from jax.sharding import PartitionSpec as P

SWEEPS = 3
MESH = pl.DeviceIdType.MESH
LANES = 128


def dot_nt(a, b):
    return lax.dot_general(a, b, (((1,), (1,)), ((), ())), preferred_element_type=jnp.float32)


def lanes_of(x, ids):
    ids = jnp.broadcast_to(ids, x.shape)
    return jnp.take_along_axis(x, ids, axis=1, mode="promise_in_bounds")


def split(x):
    high = x.astype(jnp.bfloat16)
    return high, (x - high.astype(jnp.float32)).astype(jnp.bfloat16)


def kernel(
    subs,
    regs,
    rhs_h,
    tiles_h,
    list_h,
    weights_h,
    faces_s,
    match_h,
    basis_h,
    map_h,
    inverse_h,
    solution_o,
    residual_o,
    rhs,
    tiles,
    listing,
    weights,
    match,
    basis,
    basis_t,
    own_map,
    inverse,
    dense,
    selected,
    place,
    place_s,
    ids,
    coarse,
    partial,
    solved,
    low,
    faces_out,
    faces_in,
    permuted,
    u_ref,
    r_ref,
    local_sem,
    place_sem,
    inverse_sem,
    ids_sem,
    coarse_sem,
    partial_sem,
    solved_sem,
    face_sem,
):
    rights, order = rhs.shape
    blocks = order // LANES
    listed = tiles_h.shape[0]
    held = inverse_h.shape[0]
    chips = subs // 2
    peers = chips - 1
    stride = max(regs // 4, 1)
    i, j = lax.axis_index("sub"), lax.axis_index("reg")
    chip, core = i // 2, i % 2
    mate = i + 1 - 2 * core
    after, before = (i + 1) % subs, (i + subs - 1) % subs
    apart = (i + subs - 1 + 2 * core) % subs

    def peer(m):
        return ((chip + m + 1) % chips) * 2 + core

    def send(src, dst, sems, to_sub, to_reg):
        pltpu.make_async_remote_copy(
            src_ref=src, dst_ref=dst, send_sem=sems.at[0], recv_sem=sems.at[1],
            device_id=(to_sub, to_reg), device_id_type=MESH,
        ).start()

    def waiter(ref, sems):
        return pltpu.make_async_remote_copy(
            src_ref=ref, dst_ref=ref, send_sem=sems.at[0], recv_sem=sems.at[1],
            device_id=(mate, j), device_id_type=MESH,
        )

    loads = [
        (map_h, own_map),
        (basis_h, basis),
        (rhs_h, rhs),
        (inverse_h, inverse.at[core]),
        (list_h, listing),
        (tiles_h, tiles.at[pl.ds(0, listed)]),
        (weights_h, weights),
        (match_h, match),
    ]
    loads = [pltpu.make_async_copy(a, b, local_sem.at[n]) for n, (a, b) in enumerate(loads)]
    for load in loads:
        load.start()

    with jax.named_scope("greet"):
        barrier = pltpu.get_barrier_semaphore()

        def greet(to_sub, to_reg):
            pl.semaphore_signal(barrier, inc=1, device_id=(to_sub, to_reg), device_id_type=MESH)

        def greet_peer(m, carry):
            greet(peer(m), j)
            return carry

        for by in (1, regs - 1, stride, regs - stride):
            greet(i, (j + by) % regs)
        lax.fori_loop(0, peers, greet_peer, 0)
        greet(mate, j)
        greet(apart, j)
        pl.semaphore_wait(barrier, peers + 6)

    def to_peers(src, box, sems):
        def one(m, carry):
            send(src, box.at[m], sems, peer(m), j)
            return carry

        lax.fori_loop(0, peers, one, 0)

    def send_coarse(k):
        now = lax.dot_general(
            r_ref[...].astype(jnp.bfloat16), basis[...], (((1,), (0,)), ((), ())),
            preferred_element_type=jnp.float32,
        )
        high, rest = split(now)
        coarse[k, peers, 0:rights] = high
        if coarse.shape[2] > rights:
            coarse[k, peers, rights:] = rest
        to_peers(coarse.at[k, peers], coarse.at[k], coarse_sem.at[k])

    with jax.named_scope("first_sends"):
        send(inverse_h, inverse.at[core], inverse_sem, mate, j)
        loads[0].wait()
        ids[peers] = own_map[...]
        to_peers(ids.at[peers], ids, ids_sem)
        loads[1].wait()
        loads[2].wait()
        r_ref[...] = rhs[...]
        u_ref[...] = jnp.zeros_like(u_ref)
        send_coarse(0)

    with jax.named_scope("where_tiles"):
        tiles[listed] = jnp.zeros_like(tiles[listed])
        permuted[6] = jnp.zeros_like(permuted[6])
        loads[4].wait()
        pair = listing[0:1, :] * blocks + listing[1:2, :]
        shape = (LANES, listed)
        hit = lax.broadcasted_iota(jnp.int32, shape, 0) == jnp.broadcast_to(pair, shape)
        number = lax.broadcasted_iota(jnp.int32, shape, 1)
        found = jnp.min(jnp.where(hit, number, listed), axis=1, keepdims=True)
        place[...] = jnp.broadcast_to(found, (LANES, LANES)).T[0:1]
        to_scalars = pltpu.make_async_copy(place, place_s, place_sem)
        to_scalars.start()
        for b in range(blocks):
            basis_t[:, b * LANES : (b + 1) * LANES] = basis[b * LANES : (b + 1) * LANES, :].T
        to_scalars.wait()

    with jax.named_scope("select"):
        loads[3].wait()
        waiter(inverse.at[1 - core], inverse_sem).wait_recv()
        waiter(ids.at[pl.ds(0, peers)], ids_sem).wait_recv()

        def select(s, carry):
            numbers = ids[s]
            lane, block = numbers % LANES, numbers // LANES
            for half in range(2):
                chosen = jnp.zeros((held, LANES), jnp.float32)
                for b in range(chips):
                    source = inverse[half, :, b * LANES : (b + 1) * LANES]
                    chosen = jnp.where(block == b, lanes_of(source, lane), chosen)
                high, rest = split(chosen)
                columns = pl.ds(pl.multiple_of(s * LANES, LANES), LANES)
                selected[half * held : (half + 1) * held, columns] = high
                selected[(2 + half) * held : (3 + half) * held, columns] = rest
            return carry

        lax.fori_loop(0, chips, select, 0)

    with jax.named_scope("dense"):
        loads[5].wait()

        def fill(a, carry):
            rows = pl.ds(pl.multiple_of(a * LANES, LANES), LANES)
            for b in range(blocks):
                dense[rows, b * LANES : (b + 1) * LANES] = tiles[place_s[0, a * blocks + b]]
            return carry

        lax.fori_loop(0, blocks, fill, 0)

    loads[6].wait()
    loads[7].wait()

    face_on = []
    for b in range(blocks):
        which = jnp.int32(6)
        for f in range(6):
            which = jnp.where(faces_s[0, f] == b, f, which)
        face_on.append(which)

    def sweep(k, carry):
        with jax.named_scope("wait_coarse"):
            waiter(coarse.at[k, pl.ds(0, peers)], coarse_sem.at[k]).wait_recv()
        with jax.named_scope("solve"):
            gathered = jnp.concatenate([coarse[k, s] for s in range(chips)], axis=1)
            both = dot_nt(gathered, selected[...])
            both = both[:, : 2 * held] + both[:, 2 * held :]
            mine = both[0:rights]
            if both.shape[0] > rights:
                mine = mine + both[rights:]
            partial[k, 0] = mine
            send(partial.at[k, 0], partial.at[k, 1], partial_sem.at[k], mate, j)
        with jax.named_scope("wait_mate"):
            waiter(partial.at[k, 1], partial_sem.at[k]).wait_recv()
        with jax.named_scope("send_solved"):
            solved[k, peers] = (mine + partial[k, 1]).astype(jnp.bfloat16)
            to_peers(solved.at[k, peers], solved.at[k], solved_sem.at[k])
            base = u_ref[...] + weights[...] * r_ref[...]
        with jax.named_scope("wait_solved"):
            waiter(solved.at[k, pl.ds(0, peers)], solved_sem.at[k]).wait_recv()
        with jax.named_scope("correct"):
            numbers = own_map[...]
            lane = numbers % LANES
            slot = (chip + chips - 1 - numbers // LANES) % chips
            own = jnp.zeros((rights, LANES), jnp.float32)
            for s in range(chips):
                own = jnp.where(slot == s, lanes_of(solved[k, s].astype(jnp.float32), lane), own)
            correction = lax.dot_general(
                own.astype(jnp.bfloat16), basis_t[...], (((1,), (0,)), ((), ())),
                preferred_element_type=jnp.float32,
            )
            u = base + correction
            u_ref[...] = u
            u_low = u.astype(jnp.bfloat16)
            for b in range(blocks):
                low[b] = u_low[:, b * LANES : (b + 1) * LANES]
        with jax.named_scope("send_faces"):
            for f in range(6):
                faces_out[k, f] = low[faces_s[0, f]]
            sems = face_sem.at[k]
            for f, by in ((1, 1), (0, regs - 1), (3, stride), (2, regs - stride)):
                send(faces_out.at[k, f], faces_in.at[k, f ^ 1], sems, i, (j + by) % regs)
            send(faces_out.at[k, 4], faces_in.at[k, 5], sems, before, j)
            send(faces_out.at[k, 5], faces_in.at[k, 4], sems, after, j)
        with jax.named_scope("local"):
            local = dot_nt(u_low, dense[...])
        with jax.named_scope("wait_faces"):
            waiter(faces_in.at[k], sems).wait_recv()
        with jax.named_scope("couple"):
            for f in range(6):
                permuted[f] = lanes_of(faces_in[k, f].astype(jnp.float32), match[f])
            coupling = jnp.concatenate([permuted[face_on[b]] for b in range(blocks)], axis=1)
            r_ref[...] = rhs[...] - (local - 0.5 * coupling)

        @pl.when(k < SWEEPS - 1)
        def _():
            with jax.named_scope("send_coarse"):
                send_coarse(k + 1)

        return carry

    lax.fori_loop(0, SWEEPS, sweep, 0)
    solution_o[...] = u_ref[...].astype(jnp.bfloat16)
    residual_o[...] = r_ref[...].astype(jnp.bfloat16)

    with jax.named_scope("all_sent"):
        waiter(inverse_h, inverse_sem).wait_send()
        waiter(ids.at[pl.ds(0, peers)], ids_sem).wait_send()
        for k in range(SWEEPS):
            waiter(coarse.at[k, pl.ds(0, peers)], coarse_sem.at[k]).wait_send()
            waiter(partial.at[k, 0], partial_sem.at[k]).wait_send()
            waiter(solved.at[k, pl.ds(0, peers)], solved_sem.at[k]).wait_send()
            waiter(faces_out.at[k], face_sem.at[k]).wait_send()


COARSE_ROWS = 2


def body(
    right_side,
    tiles,
    tile_list,
    weights,
    face_map,
    matching,
    coarse_basis,
    coarse_map,
    coarse_inverse,
):
    _, _, order, rights = right_side.shape
    listed, tile = tiles.shape[2:4]
    held, coarse_all = coarse_inverse.shape[1:]
    n_coarse = coarse_map.shape[2]
    subs, regs = lax.axis_size("sub"), lax.axis_size("reg")
    chips = subs // 2
    blocks = order // tile
    f32, bf16, i32 = jnp.float32, jnp.bfloat16, jnp.int32
    vmem = pltpu.VMEM
    dma = pltpu.SemaphoreType.DMA
    hbm = pl.BlockSpec(memory_space=pltpu.HBM)
    out = pl.BlockSpec(memory_space=pltpu.VMEM)
    results = pl.pallas_call(
        functools.partial(kernel, subs, regs),
        out_shape=[jax.ShapeDtypeStruct((rights, order), bf16)] * 2,
        in_specs=[hbm, hbm, hbm, hbm, pl.BlockSpec(memory_space=pltpu.SMEM), hbm, hbm, hbm, hbm],
        out_specs=[out, out],
        scratch_shapes=[
            vmem((rights, order), f32),
            vmem((listed + 1, tile, tile), bf16),
            vmem((2, listed), i32),
            vmem((1, order), f32),
            vmem((6, 1, tile), i32),
            vmem((order, n_coarse), bf16),
            vmem((n_coarse, order), bf16),
            vmem((1, n_coarse), i32),
            vmem((2, held, coarse_all), f32),
            vmem((order, order), bf16),
            vmem((4 * held, chips * n_coarse), bf16),
            vmem((1, LANES), i32),
            pltpu.SMEM((1, LANES), i32),
            vmem((chips, 1, n_coarse), i32),
            vmem((SWEEPS, chips, COARSE_ROWS * rights, n_coarse), bf16),
            vmem((SWEEPS, 2, rights, 2 * held), f32),
            vmem((SWEEPS, chips, rights, 2 * held), bf16),
            vmem((blocks, rights, tile), bf16),
            vmem((SWEEPS, 6, rights, tile), bf16),
            vmem((SWEEPS, 6, rights, tile), bf16),
            vmem((7, rights, tile), f32),
            vmem((rights, order), f32),
            vmem((rights, order), f32),
            dma((8,)),
            dma,
            dma((2,)),
            dma((2,)),
            dma((SWEEPS, 2)),
            dma((SWEEPS, 2)),
            dma((SWEEPS, 2)),
            dma((SWEEPS, 2)),
        ],
        compiler_params=pltpu.CompilerParams(
            collective_id=0, has_side_effects=True, vmem_limit_bytes=48 * 2**20
        ),
        cost_estimate=pl.CostEstimate(
            flops=SWEEPS * 2 * rights * order * (order + 2 * n_coarse),
            bytes_accessed=listed * tile * tile * 2 + held * coarse_all * 8,
            transcendentals=0,
        ),
        name="richardson",
    )(
        right_side[0, 0].T,
        tiles[0, 0],
        tile_list[0, 0].T,
        weights[0],
        face_map[0],
        matching.reshape(6, 1, tile),
        coarse_basis[0, 0],
        coarse_map[0],
        coarse_inverse[0],
    )
    return tuple(r.T.reshape(1, 1, order, rights) for r in results)


def solution(mesh):
    placed = (
        P("sub", "reg", None, None),
        P("sub", "reg", None, None, None),
        P("sub", "reg", None, None),
        P("sub", "reg", None),
        P("sub", "reg", None),
        P("sub", "reg", None, None),
        P("sub", "reg", None, None),
        P("sub", "reg", None),
        P("reg", "sub", None),
    )
    return jax.shard_map(
        body,
        mesh=mesh,
        in_specs=placed,
        out_specs=(P("sub", "reg", None, None), P("sub", "reg", None, None)),
        check_vma=False,
    )
```

```python
import functools

import jax
import jax.numpy as jnp
from jax import lax
from jax.experimental import pallas as pl
from jax.experimental.pallas import tpu as pltpu
from jax.sharding import PartitionSpec as P

SWEEPS = 3
MESH = pl.DeviceIdType.MESH
LANES = 128
GROUP = 4


def dot_nt(a, b):
    return lax.dot_general(a, b, (((1,), (1,)), ((), ())), preferred_element_type=jnp.float32)


def lanes_of(x, ids):
    ids = jnp.broadcast_to(ids, x.shape)
    return jnp.take_along_axis(x, ids, axis=1, mode="promise_in_bounds")


def split(x):
    high = x.astype(jnp.bfloat16)
    return high, (x - high.astype(jnp.float32)).astype(jnp.bfloat16)


def kernel(
    subs,
    regs,
    rhs_h,
    tiles_h,
    list_h,
    weights_h,
    faces_s,
    match_h,
    basis_h,
    map_h,
    inverse_h,
    result_o,
    rhs,
    tiles,
    listing,
    weights,
    match,
    basis,
    basis_t,
    own_map,
    inverse,
    halves,
    dense,
    selected,
    place,
    place_s,
    ids,
    coarse,
    partial,
    solved,
    low,
    faces_out,
    faces_in,
    permuted,
    u_ref,
    r_ref,
    local_sem,
    place_sem,
    inverse_sem,
    ids_sem,
    coarse_sem,
    partial_sem,
    solved_sem,
    face_sem,
):
    rights, order = rhs.shape
    blocks = order // LANES
    listed = tiles_h.shape[0]
    held = inverse_h.shape[0]
    chips = subs // 2
    groups = chips // GROUP
    stride = max(regs // 4, 1)
    i, j = lax.axis_index("sub"), lax.axis_index("reg")
    core = i % 2
    x, z = (i // 2) % GROUP, i // (2 * GROUP)
    mate = i + 1 - 2 * core
    after, before = (i + 1) % subs, (i + subs - 1) % subs
    apart = (i + subs - 1 + 2 * core) % subs

    far = (
        jnp.where(z == 0, 3, jnp.where(z == 3, 1, 2)),
        jnp.where(z == 0, 2, jnp.where(z == 3, 2, 3)),
        jnp.where(z == 0, 1, jnp.where(z == 3, 3, 1)),
    )

    def pick(n, options):
        which = options[-1]
        for m in range(len(options) - 1):
            which = jnp.where(n == m, options[m], which)
        return which

    def peer(a, b):
        return (((z + a) % groups) * GROUP + (x + b) % GROUP) * 2 + core

    def send(src, dst, sems, to_sub, to_reg):
        pltpu.make_async_remote_copy(
            src_ref=src, dst_ref=dst, send_sem=sems.at[0], recv_sem=sems.at[1],
            device_id=(to_sub, to_reg), device_id_type=MESH,
        ).start()

    def waiter(ref, sems):
        return pltpu.make_async_remote_copy(
            src_ref=ref, dst_ref=ref, send_sem=sems.at[0], recv_sem=sems.at[1],
            device_id=(mate, j), device_id_type=MESH,
        )

    loads = [
        (map_h, own_map),
        (basis_h, basis),
        (rhs_h, rhs),
        (inverse_h, inverse.at[core]),
        (list_h, listing),
        (tiles_h, tiles.at[pl.ds(0, listed)]),
        (weights_h, weights),
        (match_h, match),
    ]
    loads = [pltpu.make_async_copy(a, b, local_sem.at[n]) for n, (a, b) in enumerate(loads)]
    for load in loads:
        load.start()

    barrier = pltpu.get_barrier_semaphore()

    def greet(to_sub, to_reg):
        pl.semaphore_signal(barrier, inc=1, device_id=(to_sub, to_reg), device_id_type=MESH)

    def each_peer(act):
        def one(n, carry):
            act(pick(n // GROUP, (*far, 0)), pick(n % GROUP, (2, 1, 3, 0)))
            return carry

        lax.fori_loop(0, chips - 1, one, 0)

    for by in (1, regs - 1, stride, regs - stride):
        greet(i, (j + by) % regs)
    each_peer(lambda a, b: greet(peer(a, b), j))
    greet(mate, j)
    greet(apart, j)

    def to_peers(box, sems):
        def act(a, b):
            send(box.at[0], box.at[a * GROUP + b], sems.at[a], peer(a, b), j)

        each_peer(act)

    def arrived(box, sems, a):
        waiter(box.at[pl.ds(a * GROUP, GROUP)], sems.at[a]).wait_recv()

    def arrived_near(box, sems):
        waiter(box.at[pl.ds(1, GROUP - 1)], sems.at[0]).wait_recv()

    def sent(box, sems):
        waiter(box.at[pl.ds(1, GROUP - 1)], sems.at[0]).wait_send()
        for a in range(1, groups):
            waiter(box.at[pl.ds(a * GROUP, GROUP)], sems.at[a]).wait_send()

    def near_to_far(box, sems, act):
        arrived_near(box, sems)
        act(0)
        for a in far[::-1]:
            arrived(box, sems, a)
            act(a)

    def make_coarse(k):
        now = lax.dot_general(
            r_ref[...].astype(jnp.bfloat16), basis[...], (((1,), (0,)), ((), ())),
            preferred_element_type=jnp.float32,
        )
        high, rest = split(now)
        coarse[k, 0, 0:rights] = high
        coarse[k, 0, rights:] = rest

    loads[1].wait()
    loads[2].wait()
    r_ref[...] = rhs[...]
    u_ref[...] = jnp.zeros_like(u_ref)
    make_coarse(0)
    loads[0].wait()
    ids[0] = own_map[...]

    pl.semaphore_wait(barrier, chips + 5)
    to_peers(ids, ids_sem)
    send(inverse_h, inverse.at[core], inverse_sem, mate, j)
    to_peers(coarse.at[0], coarse_sem.at[0])

    tiles[listed] = jnp.zeros_like(tiles[listed])
    permuted[6] = jnp.zeros_like(permuted[6])
    loads[4].wait()
    pair = listing[0:1, :] * blocks + listing[1:2, :]
    shape = (LANES, listed)
    hit = lax.broadcasted_iota(jnp.int32, shape, 0) == jnp.broadcast_to(pair, shape)
    number = lax.broadcasted_iota(jnp.int32, shape, 1)
    found = jnp.min(jnp.where(hit, number, listed), axis=1, keepdims=True)
    place[...] = jnp.broadcast_to(found, (LANES, LANES)).T[0:1]
    to_scalars = pltpu.make_async_copy(place, place_s, place_sem)
    to_scalars.start()

    def keep_split(half):
        high, rest = split(inverse[half])
        rows = pl.ds(pl.multiple_of(half * held, held), held)
        halves[rows, :] = high
        rows = pl.ds(pl.multiple_of((2 + half) * held, held), held)
        halves[rows, :] = rest

    loads[3].wait()
    keep_split(core)
    waiter(inverse.at[1 - core], inverse_sem).wait_recv()
    keep_split(1 - core)

    def select(a):
        for t in range(0, GROUP, 2):
            numbers = jnp.concatenate([ids[a * GROUP + t], ids[a * GROUP + t + 1]], axis=1)
            lane, block = numbers & (LANES - 1), numbers >> 7
            shape = (LANES, 2 * LANES)
            at_lane = lax.broadcasted_iota(jnp.int32, shape, 0) == jnp.broadcast_to(lane, shape)
            at_lane = jnp.where(at_lane, 1.0, 0.0).astype(jnp.bfloat16)
            picks = []
            for b in range(chips):
                at_block = jnp.where(block == b, 1.0, 0.0).astype(jnp.bfloat16)
                picks.append(at_lane * jnp.broadcast_to(at_block, shape))
            chosen = jnp.dot(
                halves[...], jnp.concatenate(picks, axis=0), preferred_element_type=jnp.float32
            )
            selected[a, :, t * LANES : (t + 2) * LANES] = chosen.astype(jnp.bfloat16)

    near_to_far(ids, ids_sem, select)

    for b in range(blocks):
        basis_t[:, b * LANES : (b + 1) * LANES] = basis[b * LANES : (b + 1) * LANES, :].T
    to_scalars.wait()
    loads[5].wait()

    def fill(a, carry):
        rows = pl.ds(pl.multiple_of(a * LANES, LANES), LANES)
        for b in range(blocks):
            dense[rows, b * LANES : (b + 1) * LANES] = tiles[place_s[0, a * blocks + b]]
        return carry

    lax.fori_loop(0, blocks, fill, 0)
    loads[6].wait()
    loads[7].wait()

    face_on = []
    for b in range(blocks):
        which = jnp.int32(6)
        for f in range(6):
            which = jnp.where(faces_s[0, f] == b, f, which)
        face_on.append(which)

    def sweep(k, carry):
        totals = []

        def solve(a):
            gathered = jnp.concatenate([coarse[k, a * GROUP + t] for t in range(GROUP)], axis=1)
            totals.append(dot_nt(gathered, selected[a]))

        near_to_far(coarse.at[k], coarse_sem.at[k], solve)
        both = (totals[0] + totals[1]) + (totals[2] + totals[3])
        both = both[:, : 2 * held] + both[:, 2 * held :]
        mine = both[0:rights] + both[rights:]
        partial[k, 0] = mine
        send(partial.at[k, 0], partial.at[k, 1], partial_sem.at[k], mate, j)
        base = u_ref[...] + weights[...] * r_ref[...]
        waiter(partial.at[k, 1], partial_sem.at[k]).wait_recv()
        solved[k, 0] = (mine + partial[k, 1]).astype(jnp.bfloat16)
        to_peers(solved.at[k], solved_sem.at[k])

        numbers = own_map[...]
        lane, chip = numbers & (LANES - 1), numbers >> 7
        slot = ((z + groups - (chip >> 2)) & 3) * GROUP + ((x + GROUP - (chip & 3)) & 3)
        found = [jnp.zeros((rights, LANES), jnp.float32)]

        def collect(a):
            own = found[-1]
            for t in range(GROUP):
                here = lanes_of(solved[k, a * GROUP + t].astype(jnp.float32), lane)
                own = jnp.where(slot == a * GROUP + t, here, own)
            found.append(own)

        near_to_far(solved.at[k], solved_sem.at[k], collect)
        correction = lax.dot_general(
            found[-1].astype(jnp.bfloat16), basis_t[...], (((1,), (0,)), ((), ())),
            preferred_element_type=jnp.float32,
        )
        u = base + correction
        u_ref[...] = u
        u_low = u.astype(jnp.bfloat16)
        for b in range(blocks):
            low[b] = u_low[:, b * LANES : (b + 1) * LANES]
        for f in range(6):
            faces_out[k, f] = low[faces_s[0, f]]
        sems = face_sem.at[k]
        for f, by in ((1, 1), (0, regs - 1), (3, stride), (2, regs - stride)):
            send(faces_out.at[k, f], faces_in.at[k, f ^ 1], sems, i, (j + by) % regs)
        send(faces_out.at[k, 4], faces_in.at[k, 5], sems, before, j)
        send(faces_out.at[k, 5], faces_in.at[k, 4], sems, after, j)
        local = dot_nt(u_low, dense[...])
        waiter(faces_in.at[k], sems).wait_recv()
        for f in range(6):
            permuted[f] = lanes_of(faces_in[k, f].astype(jnp.float32), match[f])
        coupling = jnp.concatenate([permuted[face_on[b]] for b in range(blocks)], axis=1)
        r_ref[...] = rhs[...] - (local - 0.5 * coupling)

        @pl.when(k < SWEEPS - 1)
        def _():
            make_coarse(k + 1)
            to_peers(coarse.at[k + 1], coarse_sem.at[k + 1])

        return carry

    lax.fori_loop(0, SWEEPS, sweep, 0)
    result_o[0] = u_ref[...].astype(result_o.dtype)
    result_o[1] = r_ref[...].astype(result_o.dtype)

    waiter(inverse_h, inverse_sem).wait_send()
    sent(ids, ids_sem)
    for k in range(SWEEPS):
        sent(coarse.at[k], coarse_sem.at[k])
        waiter(partial.at[k, 0], partial_sem.at[k]).wait_send()
        sent(solved.at[k], solved_sem.at[k])
        waiter(faces_out.at[k], face_sem.at[k]).wait_send()


def body(
    right_side,
    tiles,
    tile_list,
    weights,
    face_map,
    matching,
    coarse_basis,
    coarse_map,
    coarse_inverse,
):
    _, _, order, rights = right_side.shape
    listed, tile = tiles.shape[2:4]
    held, coarse_all = coarse_inverse.shape[1:]
    n_coarse = coarse_map.shape[2]
    subs, regs = lax.axis_size("sub"), lax.axis_size("reg")
    chips = subs // 2
    blocks = order // tile
    f32, bf16, i32 = jnp.float32, jnp.bfloat16, jnp.int32
    vmem = pltpu.VMEM
    dma = pltpu.SemaphoreType.DMA
    hbm = pl.BlockSpec(memory_space=pltpu.HBM)
    result = pl.pallas_call(
        functools.partial(kernel, subs, regs),
        out_shape=jax.ShapeDtypeStruct((2, rights, order), bf16),
        in_specs=[hbm, hbm, hbm, hbm, pl.BlockSpec(memory_space=pltpu.SMEM), hbm, hbm, hbm, hbm],
        out_specs=pl.BlockSpec(memory_space=pltpu.VMEM),
        scratch_shapes=[
            vmem((rights, order), f32),
            vmem((listed + 1, tile, tile), bf16),
            vmem((2, listed), i32),
            vmem((1, order), f32),
            vmem((6, 1, tile), i32),
            vmem((order, n_coarse), bf16),
            vmem((n_coarse, order), bf16),
            vmem((1, n_coarse), i32),
            vmem((2, held, coarse_all), f32),
            vmem((4 * held, coarse_all), bf16),
            vmem((order, order), bf16),
            vmem((chips // GROUP, 4 * held, GROUP * n_coarse), bf16),
            vmem((1, LANES), i32),
            pltpu.SMEM((1, LANES), i32),
            vmem((chips, 1, n_coarse), i32),
            vmem((SWEEPS, chips, 2 * rights, n_coarse), bf16),
            vmem((SWEEPS, 2, rights, 2 * held), f32),
            vmem((SWEEPS, chips, rights, 2 * held), bf16),
            vmem((blocks, rights, tile), bf16),
            vmem((SWEEPS, 6, rights, tile), bf16),
            vmem((SWEEPS, 6, rights, tile), bf16),
            vmem((7, rights, tile), f32),
            vmem((rights, order), f32),
            vmem((rights, order), f32),
            dma((8,)),
            dma,
            dma((2,)),
            dma((GROUP, 2)),
            dma((SWEEPS, GROUP, 2)),
            dma((SWEEPS, 2)),
            dma((SWEEPS, GROUP, 2)),
            dma((SWEEPS, 2)),
        ],
        compiler_params=pltpu.CompilerParams(
            collective_id=0, has_side_effects=True, vmem_limit_bytes=56 * 2**20
        ),
        cost_estimate=pl.CostEstimate(
            flops=SWEEPS * 2 * rights * order * (order + 2 * n_coarse),
            bytes_accessed=listed * tile * tile * 2 + held * coarse_all * 8,
            transcendentals=0,
        ),
        name="richardson",
    )(
        right_side[0, 0].T,
        tiles[0, 0],
        tile_list[0, 0].T,
        weights[0],
        face_map[0],
        matching.reshape(6, 1, tile),
        coarse_basis[0, 0],
        coarse_map[0],
        coarse_inverse[0],
    )
    return tuple(result[n].T.reshape(1, 1, order, rights).astype(bf16) for n in range(2))


def solution(mesh):
    placed = (
        P("sub", "reg", None, None),
        P("sub", "reg", None, None, None),
        P("sub", "reg", None, None),
        P("sub", "reg", None),
        P("sub", "reg", None),
        P("sub", "reg", None, None),
        P("sub", "reg", None, None),
        P("sub", "reg", None),
        P("reg", "sub", None),
    )
    return jax.shard_map(
        body,
        mesh=mesh,
        in_specs=placed,
        out_specs=(P("sub", "reg", None, None), P("sub", "reg", None, None)),
        check_vma=False,
    )
```

```python
import functools

import jax
import jax.numpy as jnp
from jax import lax
from jax.experimental import pallas as pl
from jax.experimental.pallas import tpu as pltpu
from jax.sharding import PartitionSpec as P

SWEEPS = 3
MESH = pl.DeviceIdType.MESH
LANES = 128
GROUP = 4


def dot_nt(a, b):
    return lax.dot_general(a, b, (((1,), (1,)), ((), ())), preferred_element_type=jnp.float32)


def dot(a, b):
    return jnp.dot(a, b, preferred_element_type=jnp.float32)


def lanes_of(x, ids):
    ids = jnp.broadcast_to(ids, x.shape)
    return jnp.take_along_axis(x, ids, axis=1, mode="promise_in_bounds")


def split(x):
    high = x.astype(jnp.bfloat16)
    return high, (x - high.astype(jnp.float32)).astype(jnp.bfloat16)


def kernel(
    subs,
    regs,
    rhs_h,
    tiles_h,
    list_h,
    weights_h,
    faces_h,
    match_h,
    basis_h,
    map_h,
    inverse_h,
    result_o,
    rhs,
    tiles,
    listing,
    weights,
    match,
    basis,
    basis_t,
    face_basis,
    face_basis_t,
    faces_s,
    own_map,
    inverse,
    halves,
    dense,
    selected,
    place,
    place_s,
    ids,
    coarse,
    partial,
    solved,
    by_block,
    faces_out,
    faces_in,
    permuted,
    u_ref,
    r_ref,
    local_sem,
    place_sem,
    inverse_sem,
    ids_sem,
    coarse_sem,
    partial_sem,
    solved_sem,
    face_sem,
):
    rights, order = rhs.shape
    blocks = order // LANES
    listed = tiles_h.shape[0]
    held = inverse_h.shape[0]
    n_coarse = basis.shape[2]
    chips = subs // 2
    groups = chips // GROUP
    stride = max(regs // 4, 1)
    i, j = lax.axis_index("sub"), lax.axis_index("reg")
    core = i % 2
    x, z = (i // 2) % GROUP, i // (2 * GROUP)
    mate = i + 1 - 2 * core
    y = j % stride
    after, before = (i + 1) % subs, (i + subs - 1) % subs
    apart = (i + subs - 1 + 2 * core) % subs

    far = (
        jnp.where(z == 0, 3, jnp.where(z == 3, 1, 2)),
        jnp.where(z == 0, 2, jnp.where(z == 3, 2, 3)),
        jnp.where(z == 0, 1, jnp.where(z == 3, 3, 1)),
    )

    def pick(n, options):
        which = options[-1]
        for m in range(len(options) - 1):
            which = jnp.where(n == m, options[m], which)
        return which

    def peer(a, b):
        return (((z + a) % groups) * GROUP + (x + b) % GROUP) * 2 + core

    def send(src, dst, sems, to_sub, to_reg):
        pltpu.make_async_remote_copy(
            src_ref=src, dst_ref=dst, send_sem=sems.at[0], recv_sem=sems.at[1],
            device_id=(to_sub, to_reg), device_id_type=MESH,
        ).start()

    def waiter(ref, sems):
        return pltpu.make_async_remote_copy(
            src_ref=ref, dst_ref=ref, send_sem=sems.at[0], recv_sem=sems.at[1],
            device_id=(mate, j), device_id_type=MESH,
        )

    loads = [
        (map_h, own_map),
        (basis_h, basis),
        (rhs_h, rhs),
        (inverse_h, inverse.at[core]),
        (list_h, listing),
        (tiles_h, tiles.at[pl.ds(0, listed)]),
        (weights_h, weights),
        (match_h, match),
        (faces_h, faces_s),
    ]
    loads = [pltpu.make_async_copy(a, b, local_sem.at[n]) for n, (a, b) in enumerate(loads)]
    for load in loads:
        load.start()

    barrier = pltpu.get_barrier_semaphore()

    def greet(to_sub, to_reg):
        pl.semaphore_signal(barrier, inc=1, device_id=(to_sub, to_reg), device_id_type=MESH)

    def each_peer(act):
        def one(n, carry):
            act(pick(n // GROUP, (*far, 0)), pick(n % GROUP, (2, 1, 3, 0)))
            return carry

        lax.fori_loop(0, chips - 1, one, 0)

    for by in (1, regs - 1, stride, regs - stride):
        greet(i, (j + by) % regs)
    each_peer(lambda a, b: greet(peer(a, b), j))
    greet(mate, j)
    greet(apart, j)

    def to_peers(box, sems):
        def act(a, b):
            send(box.at[0], box.at[a * GROUP + b], sems.at[a], peer(a, b), j)

        each_peer(act)

    def arrived(box, sems, a):
        waiter(box.at[pl.ds(a * GROUP, GROUP)], sems.at[a]).wait_recv()

    def arrived_near(box, sems):
        waiter(box.at[pl.ds(1, GROUP - 1)], sems.at[0]).wait_recv()

    def sent(box, sems):
        waiter(box.at[pl.ds(1, GROUP - 1)], sems.at[0]).wait_send()
        for a in range(1, groups):
            waiter(box.at[pl.ds(a * GROUP, GROUP)], sems.at[a]).wait_send()

    def near_to_far(box, sems, act):
        arrived_near(box, sems)
        act(0)
        for a in far[::-1]:
            arrived(box, sems, a)
            act(a)

    def keep_coarse(k, now):
        high, rest = split(now)
        coarse[k, 0, 0:rights] = high
        coarse[k, 0, rights:] = rest

    def on_basis(r):
        return dot(r.astype(jnp.bfloat16), basis[...].reshape(order, n_coarse))

    loads[1].wait()
    loads[2].wait()
    r_ref[...] = rhs[...]
    u_ref[...] = jnp.zeros_like(u_ref)
    keep_coarse(0, on_basis(rhs[...]))
    loads[0].wait()
    ids[0] = own_map[...]

    pl.semaphore_wait(barrier, chips + 5)
    to_peers(ids, ids_sem)
    send(inverse_h, inverse.at[core], inverse_sem, mate, j)
    to_peers(coarse.at[0], coarse_sem.at[0])

    tiles[listed] = jnp.zeros_like(tiles[listed])
    permuted[6] = jnp.zeros_like(permuted[6])
    loads[4].wait()
    pair = listing[0:1, :] * blocks + listing[1:2, :]
    shape = (LANES, listed)
    hit = lax.broadcasted_iota(jnp.int32, shape, 0) == jnp.broadcast_to(pair, shape)
    number = lax.broadcasted_iota(jnp.int32, shape, 1)
    found = jnp.min(jnp.where(hit, number, listed), axis=1, keepdims=True)
    place[...] = jnp.broadcast_to(found, (LANES, LANES)).T[0:1]
    to_scalars = pltpu.make_async_copy(place, place_s, place_sem)
    to_scalars.start()

    def keep_split(half):
        high, rest = split(inverse[half])
        rows = pl.ds(pl.multiple_of(half * held, held), held)
        halves[rows, :] = high
        rows = pl.ds(pl.multiple_of((2 + half) * held, held), held)
        halves[rows, :] = rest

    loads[8].wait()
    face_on = []
    for b in range(blocks):
        which = jnp.int32(6)
        for f in range(6):
            which = jnp.where(faces_s[0, f] == b, f, which)
        face_on.append(which)
    for f in range(6):
        lanes = slice(f * LANES, (f + 1) * LANES)
        block = basis[faces_s[0, f]]
        face_basis[lanes] = block
        face_basis_t[:, lanes] = block.T
    for b in range(blocks):
        basis_t[:, b * LANES : (b + 1) * LANES] = basis[b].T
    to_scalars.wait()
    loads[5].wait()

    def fill(a, carry):
        rows = pl.ds(pl.multiple_of(a * LANES, LANES), LANES)
        for b in range(blocks):
            dense[rows, b * LANES : (b + 1) * LANES] = tiles[place_s[0, a * blocks + b]]
        return carry

    lax.fori_loop(0, blocks, fill, 0)
    loads[6].wait()
    loads[7].wait()

    loads[3].wait()
    keep_split(core)
    waiter(inverse.at[1 - core], inverse_sem).wait_recv()
    keep_split(1 - core)

    def select(a):
        for t in range(0, GROUP, 2):
            numbers = jnp.concatenate([ids[a * GROUP + t], ids[a * GROUP + t + 1]], axis=1)
            lane, block = numbers & (LANES - 1), numbers >> 7
            shape = (LANES, 2 * LANES)
            at_lane = lax.broadcasted_iota(jnp.int32, shape, 0) == jnp.broadcast_to(lane, shape)
            at_lane = jnp.where(at_lane, 1.0, 0.0).astype(jnp.bfloat16)
            picks = []
            for b in range(chips):
                at_block = jnp.where(block == b, 1.0, 0.0).astype(jnp.bfloat16)
                picks.append(at_lane * jnp.broadcast_to(at_block, shape))
            chosen = jnp.dot(
                halves[...], jnp.concatenate(picks, axis=0), preferred_element_type=jnp.float32
            )
            selected[a, :, t * LANES : (t + 2) * LANES] = chosen.astype(jnp.bfloat16)

    near_to_far(ids, ids_sem, select)
    waiter(inverse_h, inverse_sem).wait_send()
    sent(ids, ids_sem)

    def faces_of(field):
        for b in range(blocks):
            by_block[b] = field[:, b * LANES : (b + 1) * LANES]
        return jnp.concatenate([by_block[faces_s[0, f]] for f in range(6)], axis=1)

    def sweep(k, carry):
        totals = []

        def solve(a):
            gathered = jnp.concatenate([coarse[k, a * GROUP + t] for t in range(GROUP)], axis=1)
            totals.append(dot_nt(gathered, selected[a]))

        near_to_far(coarse.at[k], coarse_sem.at[k], solve)
        both = (totals[0] + totals[1]) + (totals[2] + totals[3])
        both = both[:, : 2 * held] + both[:, 2 * held :]
        mine = both[0:rights] + both[rights:]
        partial[k, 0] = mine
        send(partial.at[k, 0], partial.at[k, 1], partial_sem.at[k], mate, j)
        base = u_ref[...] + weights[...] * r_ref[...]
        base_faces = faces_of(base)
        waiter(partial.at[k, 1], partial_sem.at[k]).wait_recv()
        solved[k, 0] = (mine + partial[k, 1]).astype(jnp.bfloat16)
        to_peers(solved.at[k], solved_sem.at[k])

        numbers = own_map[...]
        lane, chip = numbers & (LANES - 1), numbers >> 7
        slot = ((z + groups - (chip >> 2)) & 3) * GROUP + ((x + GROUP - (chip & 3)) & 3)
        found = [jnp.zeros((rights, LANES), jnp.float32)]

        def collect(a):
            own = found[-1]
            for t in range(GROUP):
                here = lanes_of(solved[k, a * GROUP + t].astype(jnp.float32), lane)
                own = jnp.where(slot == a * GROUP + t, here, own)
            found.append(own)

        near_to_far(solved.at[k], solved_sem.at[k], collect)
        own = found[-1].astype(jnp.bfloat16)
        u_faces = (base_faces + dot(own, face_basis_t[...])).astype(jnp.bfloat16)
        for f in range(6):
            faces_out[k, f] = u_faces[:, f * LANES : (f + 1) * LANES]
        sems = face_sem.at[k]

        def send_face(n, carry):
            f = pick(n, (pick(y, (0, 3, 3, 1)), pick(y, (3, 2, 2, 3)), pick(y, (2, 1, 1, 2)), pick(y, (1, 0, 0, 0))))
            by = pick(f, (regs - 1, 1, regs - stride, stride))
            send(faces_out.at[k, f], faces_in.at[k, f + 1 - 2 * (f % 2)], sems, i, (j + by) % regs)
            return carry

        lax.fori_loop(0, 4, send_face, 0)
        send(faces_out.at[k, 4], faces_in.at[k, 5], sems, before, j)
        send(faces_out.at[k, 5], faces_in.at[k, 4], sems, after, j)

        u = base + dot(own, basis_t[...])
        u_ref[...] = u
        here = rhs[...] - dot_nt(u.astype(jnp.bfloat16), dense[...])
        here_faces = faces_of(here)
        inside = [
            jnp.where(face_on[b] == 6, here[:, b * LANES : (b + 1) * LANES], 0.0) for b in range(blocks)
        ]
        coarse_inside = on_basis(jnp.concatenate(inside, axis=1))
        sent(coarse.at[k], coarse_sem.at[k])
        waiter(partial.at[k, 0], partial_sem.at[k]).wait_send()
        sent(solved.at[k], solved_sem.at[k])

        waiter(faces_in.at[k], sems).wait_recv()
        coupling = [0.5 * lanes_of(faces_in[k, f].astype(jnp.float32), match[f]) for f in range(6)]

        @pl.when(k < SWEEPS - 1)
        def _():
            r_faces = here_faces + jnp.concatenate(coupling, axis=1)
            keep_coarse(k + 1, coarse_inside + dot(r_faces.astype(jnp.bfloat16), face_basis[...]))
            to_peers(coarse.at[k + 1], coarse_sem.at[k + 1])

        for f in range(6):
            permuted[f] = coupling[f]
        r_ref[...] = here + jnp.concatenate([permuted[face_on[b]] for b in range(blocks)], axis=1)
        return carry

    lax.fori_loop(0, SWEEPS, sweep, 0)
    result_o[0] = u_ref[...].astype(result_o.dtype)
    result_o[1] = r_ref[...].astype(result_o.dtype)

    for k in range(SWEEPS):
        waiter(faces_out.at[k], face_sem.at[k]).wait_send()


def body(
    right_side,
    tiles,
    tile_list,
    weights,
    face_map,
    matching,
    coarse_basis,
    coarse_map,
    coarse_inverse,
):
    _, _, order, rights = right_side.shape
    listed, tile = tiles.shape[2:4]
    held, coarse_all = coarse_inverse.shape[1:]
    n_coarse = coarse_map.shape[2]
    subs, regs = lax.axis_size("sub"), lax.axis_size("reg")
    chips = subs // 2
    blocks = order // tile
    f32, bf16, i32 = jnp.float32, jnp.bfloat16, jnp.int32
    vmem = pltpu.VMEM
    dma = pltpu.SemaphoreType.DMA
    hbm = pl.BlockSpec(memory_space=pltpu.HBM)
    result = pl.pallas_call(
        functools.partial(kernel, subs, regs),
        out_shape=pltpu.VMEM((2, rights, order), bf16),
        in_specs=[hbm] * 9,
        out_specs=pl.BlockSpec(memory_space=pltpu.VMEM),
        scratch_shapes=[
            vmem((rights, order), f32),
            vmem((listed + 1, tile, tile), bf16),
            vmem((2, listed), i32),
            vmem((1, order), f32),
            vmem((6, 1, tile), i32),
            vmem((blocks, tile, n_coarse), bf16),
            vmem((n_coarse, order), bf16),
            vmem((6 * tile, n_coarse), bf16),
            vmem((n_coarse, 6 * tile), bf16),
            pltpu.SMEM((1, 6), i32),
            vmem((1, n_coarse), i32),
            vmem((2, held, coarse_all), f32),
            vmem((4 * held, coarse_all), bf16),
            vmem((order, order), bf16),
            vmem((chips // GROUP, 4 * held, GROUP * n_coarse), bf16),
            vmem((1, LANES), i32),
            pltpu.SMEM((1, LANES), i32),
            vmem((chips, 1, n_coarse), i32),
            vmem((SWEEPS, chips, 2 * rights, n_coarse), bf16),
            vmem((SWEEPS, 2, rights, 2 * held), f32),
            vmem((SWEEPS, chips, rights, 2 * held), bf16),
            vmem((blocks, rights, tile), f32),
            vmem((SWEEPS, 6, rights, tile), bf16),
            vmem((SWEEPS, 6, rights, tile), bf16),
            vmem((7, rights, tile), f32),
            vmem((rights, order), f32),
            vmem((rights, order), f32),
            dma((9,)),
            dma,
            dma((2,)),
            dma((GROUP, 2)),
            dma((SWEEPS, GROUP, 2)),
            dma((SWEEPS, 2)),
            dma((SWEEPS, GROUP, 2)),
            dma((SWEEPS, 2)),
        ],
        compiler_params=pltpu.CompilerParams(
            collective_id=0, has_side_effects=True, vmem_limit_bytes=56 * 2**20
        ),
        cost_estimate=pl.CostEstimate(
            flops=SWEEPS * 2 * rights * order * (order + 2 * n_coarse),
            bytes_accessed=listed * tile * tile * 2 + held * coarse_all * 8,
            transcendentals=0,
        ),
        name="richardson",
    )(
        right_side[0, 0].T,
        tiles[0, 0],
        tile_list[0, 0].T,
        weights[0],
        face_map[0],
        matching.reshape(6, 1, tile),
        coarse_basis.reshape(blocks, tile, n_coarse),
        coarse_map[0],
        coarse_inverse[0],
    )
    return tuple(result[n].T.reshape(1, 1, order, rights).astype(bf16) for n in range(2))


def solution(mesh):
    placed = (
        P("sub", "reg", None, None),
        P("sub", "reg", None, None, None),
        P("sub", "reg", None, None),
        P("sub", "reg", None),
        P("sub", "reg", None),
        P("sub", "reg", None, None),
        P("sub", "reg", None, None),
        P("sub", "reg", None),
        P("reg", "sub", None),
    )
    return jax.shard_map(
        body,
        mesh=mesh,
        in_specs=placed,
        out_specs=(P("sub", "reg", None, None), P("sub", "reg", None, None)),
        check_vma=False,
    )
```

```python
import functools

import jax
import jax.numpy as jnp
from jax import lax
from jax.experimental import pallas as pl
from jax.experimental.pallas import tpu as pltpu
from jax.sharding import PartitionSpec as P

SWEEPS = 3
MESH = pl.DeviceIdType.MESH
LANES = 128
GROUP = 4


def dot_nt(a, b):
    return lax.dot_general(a, b, (((1,), (1,)), ((), ())), preferred_element_type=jnp.float32)


def dot(a, b):
    return jnp.dot(a, b, preferred_element_type=jnp.float32)


def lanes_of(x, ids):
    ids = jnp.broadcast_to(ids, x.shape)
    return jnp.take_along_axis(x, ids, axis=1, mode="promise_in_bounds")


def split(x):
    high = x.astype(jnp.bfloat16)
    return high, (x - high.astype(jnp.float32)).astype(jnp.bfloat16)


def kernel(
    subs,
    regs,
    rhs_h,
    tiles_h,
    list_h,
    weights_h,
    faces_h,
    match_h,
    basis_h,
    map_h,
    inverse_h,
    result_o,
    rhs,
    tiles,
    listing,
    weights,
    match,
    basis,
    basis_t,
    face_basis,
    face_basis_t,
    faces_s,
    own_map,
    inverse,
    halves,
    dense,
    selected,
    place,
    place_s,
    ids,
    coarse,
    partial,
    solved,
    by_block,
    faces_out,
    faces_in,
    permuted,
    u_ref,
    r_ref,
    local_sem,
    place_sem,
    inverse_sem,
    ids_sem,
    coarse_sem,
    partial_sem,
    solved_sem,
    face_sem,
):
    rights, order = rhs.shape
    blocks = order // LANES
    listed = tiles_h.shape[0]
    held = inverse_h.shape[0]
    n_coarse = basis.shape[2]
    chips = subs // 2
    groups = chips // GROUP
    stride = max(regs // 4, 1)
    i, j = lax.axis_index("sub"), lax.axis_index("reg")
    core = i % 2
    x, z = (i // 2) % GROUP, i // (2 * GROUP)
    mate = i + 1 - 2 * core
    y = j % stride
    after, before = (i + 1) % subs, (i + subs - 1) % subs
    apart = (i + subs - 1 + 2 * core) % subs

    far = (
        jnp.where(z == 0, 3, jnp.where(z == 3, 1, 2)),
        jnp.where(z == 0, 2, jnp.where(z == 3, 2, 3)),
        jnp.where(z == 0, 1, jnp.where(z == 3, 3, 1)),
    )

    def pick(n, options):
        which = options[-1]
        for m in range(len(options) - 1):
            which = jnp.where(n == m, options[m], which)
        return which

    def peer(a, b):
        return (((z + a) % groups) * GROUP + (x + b) % GROUP) * 2 + core

    def send(src, dst, sems, to_sub, to_reg):
        pltpu.make_async_remote_copy(
            src_ref=src, dst_ref=dst, send_sem=sems.at[0], recv_sem=sems.at[1],
            device_id=(to_sub, to_reg), device_id_type=MESH,
        ).start()

    def waiter(ref, sems):
        return pltpu.make_async_remote_copy(
            src_ref=ref, dst_ref=ref, send_sem=sems.at[0], recv_sem=sems.at[1],
            device_id=(mate, j), device_id_type=MESH,
        )

    loads = [
        (map_h, own_map),
        (basis_h, basis),
        (rhs_h, rhs),
        (inverse_h, inverse.at[core]),
        (list_h, listing),
        (tiles_h, tiles.at[pl.ds(0, listed)]),
        (weights_h, weights),
        (match_h, match),
        (faces_h, faces_s),
    ]
    loads = [pltpu.make_async_copy(a, b, local_sem.at[n]) for n, (a, b) in enumerate(loads)]
    for load in loads:
        load.start()

    barrier = pltpu.get_barrier_semaphore()

    def greet(to_sub, to_reg):
        pl.semaphore_signal(barrier, inc=1, device_id=(to_sub, to_reg), device_id_type=MESH)

    def each_peer(act):
        def one(n, carry):
            act(pick(n // GROUP, (*far, 0)), pick(n % GROUP, (2, 1, 3, 0)))
            return carry

        lax.fori_loop(0, chips - 1, one, 0)

    for by in (1, regs - 1, stride, regs - stride):
        greet(i, (j + by) % regs)
    each_peer(lambda a, b: greet(peer(a, b), j))
    greet(mate, j)
    greet(apart, j)

    def to_peers(box, sems, grouped=False):
        def act(a, b):
            send(box.at[0], box.at[a * GROUP + b], sems.at[a] if grouped else sems, peer(a, b), j)

        each_peer(act)

    def arrived(box, sems, a):
        waiter(box.at[pl.ds(a * GROUP, GROUP)], sems.at[a]).wait_recv()

    def arrived_near(box, sems):
        waiter(box.at[pl.ds(1, GROUP - 1)], sems.at[0]).wait_recv()

    def sent(box, sems):
        waiter(box.at[pl.ds(1, GROUP - 1)], sems.at[0]).wait_send()
        for a in range(1, groups):
            waiter(box.at[pl.ds(a * GROUP, GROUP)], sems.at[a]).wait_send()

    def near_to_far(box, sems, act):
        arrived_near(box, sems)
        act(0)
        for a in far[::-1]:
            arrived(box, sems, a)
            act(a)

    def keep_coarse(k, now):
        high, rest = split(now)
        coarse[k, 0, 0:rights] = high
        coarse[k, 0, rights:] = rest

    def on_basis(r):
        return dot(r.astype(jnp.bfloat16), basis[...].reshape(order, n_coarse))

    loads[0].wait()
    ids[0] = own_map[...]
    pl.semaphore_wait(barrier, chips + 5)
    to_peers(ids, ids_sem, True)
    send(inverse_h, inverse.at[core], inverse_sem, mate, j)
    loads[1].wait()
    loads[2].wait()
    keep_coarse(0, on_basis(rhs[...]))
    to_peers(coarse.at[0], coarse_sem.at[0])
    r_ref[...] = rhs[...]
    u_ref[...] = jnp.zeros_like(u_ref)

    tiles[listed] = jnp.zeros_like(tiles[listed])
    permuted[6] = jnp.zeros_like(permuted[6])
    loads[4].wait()
    pair = listing[0:1, :] * blocks + listing[1:2, :]
    shape = (LANES, listed)
    hit = lax.broadcasted_iota(jnp.int32, shape, 0) == jnp.broadcast_to(pair, shape)
    number = lax.broadcasted_iota(jnp.int32, shape, 1)
    found = jnp.min(jnp.where(hit, number, listed), axis=1, keepdims=True)
    place[...] = jnp.broadcast_to(found, (LANES, LANES)).T[0:1]
    to_scalars = pltpu.make_async_copy(place, place_s, place_sem)
    to_scalars.start()

    def keep_split(half):
        high, rest = split(inverse[half])
        rows = pl.ds(pl.multiple_of(half * held, held), held)
        halves[rows, :] = high
        rows = pl.ds(pl.multiple_of((2 + half) * held, held), held)
        halves[rows, :] = rest

    loads[8].wait()
    face_on = []
    for b in range(blocks):
        which = jnp.int32(6)
        for f in range(6):
            which = jnp.where(faces_s[0, f] == b, f, which)
        face_on.append(which)
    for f in range(6):
        lanes = slice(f * LANES, (f + 1) * LANES)
        block = basis[faces_s[0, f]]
        face_basis[lanes] = block
        face_basis_t[:, lanes] = block.T
    for b in range(blocks):
        basis_t[:, b * LANES : (b + 1) * LANES] = basis[b].T
    to_scalars.wait()
    loads[5].wait()

    def fill(a, carry):
        rows = pl.ds(pl.multiple_of(a * LANES, LANES), LANES)
        for b in range(blocks):
            dense[rows, b * LANES : (b + 1) * LANES] = tiles[place_s[0, a * blocks + b]]
        return carry

    lax.fori_loop(0, blocks, fill, 0)
    loads[6].wait()
    loads[7].wait()

    loads[3].wait()
    keep_split(core)
    waiter(inverse.at[1 - core], inverse_sem).wait_recv()
    keep_split(1 - core)

    def select(a):
        for t in range(0, GROUP, 2):
            numbers = jnp.concatenate([ids[a * GROUP + t], ids[a * GROUP + t + 1]], axis=1)
            lane, block = numbers & (LANES - 1), numbers >> 7
            shape = (LANES, 2 * LANES)
            at_lane = lax.broadcasted_iota(jnp.int32, shape, 0) == jnp.broadcast_to(lane, shape)
            at_lane = jnp.where(at_lane, 1.0, 0.0).astype(jnp.bfloat16)
            picks = []
            for b in range(chips):
                at_block = jnp.where(block == b, 1.0, 0.0).astype(jnp.bfloat16)
                picks.append(at_lane * jnp.broadcast_to(at_block, shape))
            chosen = jnp.dot(
                halves[...], jnp.concatenate(picks, axis=0), preferred_element_type=jnp.float32
            )
            start = pl.multiple_of((a * GROUP + t) * LANES, 2 * LANES)
            selected[:, pl.ds(start, 2 * LANES)] = chosen.astype(jnp.bfloat16)

    near_to_far(ids, ids_sem, select)
    waiter(inverse_h, inverse_sem).wait_send()
    sent(ids, ids_sem)

    def faces_of(field):
        for b in range(blocks):
            by_block[b] = field[:, b * LANES : (b + 1) * LANES]
        return jnp.concatenate([by_block[faces_s[0, f]] for f in range(6)], axis=1)

    def sweep(k, carry):
        waiter(coarse.at[k, pl.ds(1, chips - 1)], coarse_sem.at[k]).wait_recv()
        gathered = jnp.concatenate([coarse[k, s] for s in range(chips)], axis=1)
        both = dot_nt(gathered, selected[...])
        both = both[:, : 2 * held] + both[:, 2 * held :]
        mine = both[0:rights] + both[rights:]
        partial[k, 0] = mine
        send(partial.at[k, 0], partial.at[k, 1], partial_sem.at[k], mate, j)
        base = u_ref[...] + weights[...] * r_ref[...]
        base_faces = faces_of(base)
        waiter(partial.at[k, 1], partial_sem.at[k]).wait_recv()
        solved[k, 0] = (mine + partial[k, 1]).astype(jnp.bfloat16)
        to_peers(solved.at[k], solved_sem.at[k])

        numbers = own_map[...]
        lane, chip = numbers & (LANES - 1), numbers >> 7
        slot = ((z + groups - (chip >> 2)) & 3) * GROUP + ((x + GROUP - (chip & 3)) & 3)
        waiter(solved.at[k, pl.ds(1, chips - 1)], solved_sem.at[k]).wait_recv()
        own = jnp.zeros((rights, LANES), jnp.float32)
        for s in range(chips):
            own = jnp.where(slot == s, lanes_of(solved[k, s].astype(jnp.float32), lane), own)
        own = own.astype(jnp.bfloat16)
        u_faces = (base_faces + dot(own, face_basis_t[...])).astype(jnp.bfloat16)
        for f in range(6):
            faces_out[k, f] = u_faces[:, f * LANES : (f + 1) * LANES]
        sems = face_sem.at[k]

        def send_face(n, carry):
            f = pick(n, (pick(y, (0, 3, 3, 1)), pick(y, (3, 2, 2, 3)), pick(y, (2, 1, 1, 2)), pick(y, (1, 0, 0, 0))))
            by = pick(f, (regs - 1, 1, regs - stride, stride))
            send(faces_out.at[k, f], faces_in.at[k, f + 1 - 2 * (f % 2)], sems, i, (j + by) % regs)
            return carry

        lax.fori_loop(0, 4, send_face, 0)
        send(faces_out.at[k, 4], faces_in.at[k, 5], sems, before, j)
        send(faces_out.at[k, 5], faces_in.at[k, 4], sems, after, j)

        u = base + dot(own, basis_t[...])
        u_ref[...] = u
        here = rhs[...] - dot_nt(u.astype(jnp.bfloat16), dense[...])
        here_faces = faces_of(here)
        inside = [
            jnp.where(face_on[b] == 6, here[:, b * LANES : (b + 1) * LANES], 0.0) for b in range(blocks)
        ]
        coarse_inside = on_basis(jnp.concatenate(inside, axis=1))
        waiter(coarse.at[k, pl.ds(1, chips - 1)], coarse_sem.at[k]).wait_send()
        waiter(partial.at[k, 0], partial_sem.at[k]).wait_send()
        waiter(solved.at[k, pl.ds(1, chips - 1)], solved_sem.at[k]).wait_send()

        waiter(faces_in.at[k], sems).wait_recv()
        coupling = [0.5 * lanes_of(faces_in[k, f].astype(jnp.float32), match[f]) for f in range(6)]

        @pl.when(k < SWEEPS - 1)
        def _():
            r_faces = here_faces + jnp.concatenate(coupling, axis=1)
            keep_coarse(k + 1, coarse_inside + dot(r_faces.astype(jnp.bfloat16), face_basis[...]))
            to_peers(coarse.at[k + 1], coarse_sem.at[k + 1])

        for f in range(6):
            permuted[f] = coupling[f]
        r_ref[...] = here + jnp.concatenate([permuted[face_on[b]] for b in range(blocks)], axis=1)
        return carry

    lax.fori_loop(0, SWEEPS, sweep, 0)
    result_o[0] = u_ref[...].astype(result_o.dtype)
    result_o[1] = r_ref[...].astype(result_o.dtype)

    for k in range(SWEEPS):
        waiter(faces_out.at[k], face_sem.at[k]).wait_send()


def body(
    right_side,
    tiles,
    tile_list,
    weights,
    face_map,
    matching,
    coarse_basis,
    coarse_map,
    coarse_inverse,
):
    _, _, order, rights = right_side.shape
    listed, tile = tiles.shape[2:4]
    held, coarse_all = coarse_inverse.shape[1:]
    n_coarse = coarse_map.shape[2]
    subs, regs = lax.axis_size("sub"), lax.axis_size("reg")
    chips = subs // 2
    blocks = order // tile
    f32, bf16, i32 = jnp.float32, jnp.bfloat16, jnp.int32
    vmem = pltpu.VMEM
    dma = pltpu.SemaphoreType.DMA
    hbm = pl.BlockSpec(memory_space=pltpu.HBM)
    result = pl.pallas_call(
        functools.partial(kernel, subs, regs),
        out_shape=pltpu.VMEM((2, rights, order), bf16),
        in_specs=[hbm] * 9,
        out_specs=pl.BlockSpec(memory_space=pltpu.VMEM),
        scratch_shapes=[
            vmem((rights, order), f32),
            vmem((listed + 1, tile, tile), bf16),
            vmem((2, listed), i32),
            vmem((1, order), f32),
            vmem((6, 1, tile), i32),
            vmem((blocks, tile, n_coarse), bf16),
            vmem((n_coarse, order), bf16),
            vmem((6 * tile, n_coarse), bf16),
            vmem((n_coarse, 6 * tile), bf16),
            pltpu.SMEM((1, 6), i32),
            vmem((1, n_coarse), i32),
            vmem((2, held, coarse_all), f32),
            vmem((4 * held, coarse_all), bf16),
            vmem((order, order), bf16),
            vmem((4 * held, chips * n_coarse), bf16),
            vmem((1, LANES), i32),
            pltpu.SMEM((1, LANES), i32),
            vmem((chips, 1, n_coarse), i32),
            vmem((SWEEPS, chips, 2 * rights, n_coarse), bf16),
            vmem((SWEEPS, 2, rights, 2 * held), f32),
            vmem((SWEEPS, chips, rights, 2 * held), bf16),
            vmem((blocks, rights, tile), f32),
            vmem((SWEEPS, 6, rights, tile), bf16),
            vmem((SWEEPS, 6, rights, tile), bf16),
            vmem((7, rights, tile), f32),
            vmem((rights, order), f32),
            vmem((rights, order), f32),
            dma((9,)),
            dma,
            dma((2,)),
            dma((GROUP, 2)),
            dma((SWEEPS, 2)),
            dma((SWEEPS, 2)),
            dma((SWEEPS, 2)),
            dma((SWEEPS, 2)),
        ],
        compiler_params=pltpu.CompilerParams(
            collective_id=0, has_side_effects=True, vmem_limit_bytes=56 * 2**20
        ),
        cost_estimate=pl.CostEstimate(
            flops=SWEEPS * 2 * rights * order * (order + 2 * n_coarse),
            bytes_accessed=listed * tile * tile * 2 + held * coarse_all * 8,
            transcendentals=0,
        ),
        name="richardson",
    )(
        right_side[0, 0].T,
        tiles[0, 0],
        tile_list[0, 0].T,
        weights[0],
        face_map[0],
        matching.reshape(6, 1, tile),
        coarse_basis.reshape(blocks, tile, n_coarse),
        coarse_map[0],
        coarse_inverse[0],
    )
    return tuple(result[n].T.reshape(1, 1, order, rights).astype(bf16) for n in range(2))


def solution(mesh):
    placed = (
        P("sub", "reg", None, None),
        P("sub", "reg", None, None, None),
        P("sub", "reg", None, None),
        P("sub", "reg", None),
        P("sub", "reg", None),
        P("sub", "reg", None, None),
        P("sub", "reg", None, None),
        P("sub", "reg", None),
        P("reg", "sub", None),
    )
    return jax.shard_map(
        body,
        mesh=mesh,
        in_specs=placed,
        out_specs=(P("sub", "reg", None, None), P("sub", "reg", None, None)),
        check_vma=False,
    )
```

```python
import functools

import jax
import jax.numpy as jnp
from jax import lax
from jax.experimental import pallas as pl
from jax.experimental.pallas import tpu as pltpu
from jax.sharding import PartitionSpec as P

SWEEPS = 3
MESH = pl.DeviceIdType.MESH
LANES = 128
GROUP = 4


def dot_nt(a, b):
    return lax.dot_general(a, b, (((1,), (1,)), ((), ())), preferred_element_type=jnp.float32)


def dot(a, b):
    return jnp.dot(a, b, preferred_element_type=jnp.float32)


def lanes_of(x, ids):
    ids = jnp.broadcast_to(ids, x.shape)
    return jnp.take_along_axis(x, ids, axis=1, mode="promise_in_bounds")


def split(x):
    high = x.astype(jnp.bfloat16)
    return high, (x - high.astype(jnp.float32)).astype(jnp.bfloat16)


def kernel(
    subs,
    regs,
    rhs_h,
    tiles_h,
    list_h,
    weights_h,
    faces_h,
    match_h,
    basis_h,
    map_h,
    inverse_h,
    result_o,
    rhs,
    tiles,
    listing,
    weights,
    match,
    basis,
    basis_t,
    face_basis,
    face_basis_t,
    faces_s,
    own_map,
    inverse,
    halves,
    dense,
    selected,
    place,
    place_s,
    ids,
    coarse,
    partial,
    solved,
    by_block,
    faces_out,
    faces_in,
    permuted,
    u_ref,
    r_ref,
    local_sem,
    place_sem,
    inverse_sem,
    ids_sem,
    coarse_sem,
    partial_sem,
    solved_sem,
    face_sem,
):
    rights, order = rhs.shape
    blocks = order // LANES
    listed = tiles_h.shape[0]
    held = inverse_h.shape[0]
    n_coarse = basis.shape[2]
    chips = subs // 2
    groups = chips // GROUP
    stride = max(regs // 4, 1)
    i, j = lax.axis_index("sub"), lax.axis_index("reg")
    core = i % 2
    x, z = (i // 2) % GROUP, i // (2 * GROUP)
    mate = i + 1 - 2 * core
    after, before = (i + 1) % subs, (i + subs - 1) % subs
    apart = (i + subs - 1 + 2 * core) % subs

    far = (
        jnp.where(z == 0, 3, jnp.where(z == 3, 1, 2)),
        jnp.where(z == 0, 2, jnp.where(z == 3, 2, 3)),
        jnp.where(z == 0, 1, jnp.where(z == 3, 3, 1)),
    )

    def pick(n, options):
        which = options[-1]
        for m in range(len(options) - 1):
            which = jnp.where(n == m, options[m], which)
        return which

    def peer(a, b):
        return (((z + a) % groups) * GROUP + (x + b) % GROUP) * 2 + core

    def send(src, dst, sems, to_sub, to_reg):
        pltpu.make_async_remote_copy(
            src_ref=src, dst_ref=dst, send_sem=sems.at[0], recv_sem=sems.at[1],
            device_id=(to_sub, to_reg), device_id_type=MESH,
        ).start()

    def waiter(ref, sems):
        return pltpu.make_async_remote_copy(
            src_ref=ref, dst_ref=ref, send_sem=sems.at[0], recv_sem=sems.at[1],
            device_id=(mate, j), device_id_type=MESH,
        )

    loads = [
        (map_h, own_map),
        (basis_h, basis),
        (rhs_h, rhs),
        (inverse_h, inverse.at[core]),
        (list_h, listing),
        (tiles_h, tiles.at[pl.ds(0, listed)]),
        (weights_h, weights),
        (match_h, match),
        (faces_h, faces_s),
    ]
    loads = [pltpu.make_async_copy(a, b, local_sem.at[n]) for n, (a, b) in enumerate(loads)]
    for load in loads:
        load.start()

    barrier = pltpu.get_barrier_semaphore()

    def greet(to_sub, to_reg):
        pl.semaphore_signal(barrier, inc=1, device_id=(to_sub, to_reg), device_id_type=MESH)

    def each_peer(act):
        def one(n, carry):
            act(pick(n // GROUP, (*far, 0)), pick(n % GROUP, (2, 1, 3, 0)))
            return carry

        lax.fori_loop(0, chips - 1, one, 0)

    for by in (1, regs - 1, stride, regs - stride):
        greet(i, (j + by) % regs)
    each_peer(lambda a, b: greet(peer(a, b), j))
    greet(mate, j)
    greet(apart, j)

    def to_peers(box, sems, grouped=False):
        def act(a, b):
            send(box.at[0], box.at[a * GROUP + b], sems.at[a] if grouped else sems, peer(a, b), j)

        each_peer(act)

    def arrived(box, sems, a):
        waiter(box.at[pl.ds(a * GROUP, GROUP)], sems.at[a]).wait_recv()

    def arrived_near(box, sems):
        waiter(box.at[pl.ds(1, GROUP - 1)], sems.at[0]).wait_recv()

    def sent(box, sems):
        waiter(box.at[pl.ds(1, GROUP - 1)], sems.at[0]).wait_send()
        for a in range(1, groups):
            waiter(box.at[pl.ds(a * GROUP, GROUP)], sems.at[a]).wait_send()

    def near_to_far(box, sems, act):
        arrived_near(box, sems)
        act(0)
        for a in far[::-1]:
            arrived(box, sems, a)
            act(a)

    def keep_coarse(k, now):
        high, rest = split(now)
        coarse[k, 0, 0:rights] = high
        coarse[k, 0, rights:] = rest

    def on_basis(r):
        return dot(r.astype(jnp.bfloat16), basis[...].reshape(order, n_coarse))

    loads[0].wait()
    ids[0] = own_map[...]
    pl.semaphore_wait(barrier, chips + 5)
    to_peers(ids, ids_sem, True)
    send(inverse_h, inverse.at[core], inverse_sem, mate, j)
    loads[1].wait()
    loads[2].wait()
    keep_coarse(0, on_basis(rhs[...]))
    to_peers(coarse.at[0], coarse_sem.at[0])
    r_ref[...] = rhs[...]
    u_ref[...] = jnp.zeros_like(u_ref)

    tiles[listed] = jnp.zeros_like(tiles[listed])
    permuted[6] = jnp.zeros_like(permuted[6])
    loads[4].wait()
    pair = listing[0:1, :] * blocks + listing[1:2, :]
    shape = (LANES, listed)
    hit = lax.broadcasted_iota(jnp.int32, shape, 0) == jnp.broadcast_to(pair, shape)
    number = lax.broadcasted_iota(jnp.int32, shape, 1)
    found = jnp.min(jnp.where(hit, number, listed), axis=1, keepdims=True)
    place[...] = jnp.broadcast_to(found, (LANES, LANES)).T[0:1]
    to_scalars = pltpu.make_async_copy(place, place_s, place_sem)
    to_scalars.start()

    def keep_split(half):
        high, rest = split(inverse[half])
        rows = pl.ds(pl.multiple_of(half * held, held), held)
        halves[rows, :] = high
        rows = pl.ds(pl.multiple_of((2 + half) * held, held), held)
        halves[rows, :] = rest

    loads[8].wait()
    face_on = []
    for b in range(blocks):
        which = jnp.int32(6)
        for f in range(6):
            which = jnp.where(faces_s[0, f] == b, f, which)
        face_on.append(which)
    for f in range(6):
        lanes = slice(f * LANES, (f + 1) * LANES)
        block = basis[faces_s[0, f]]
        face_basis[lanes] = block
        face_basis_t[:, lanes] = block.T
    for b in range(blocks):
        basis_t[:, b * LANES : (b + 1) * LANES] = basis[b].T
    to_scalars.wait()
    loads[5].wait()

    def fill(a, carry):
        rows = pl.ds(pl.multiple_of(a * LANES, LANES), LANES)
        for b in range(blocks):
            dense[rows, b * LANES : (b + 1) * LANES] = tiles[place_s[0, a * blocks + b]]
        return carry

    lax.fori_loop(0, blocks, fill, 0)
    loads[6].wait()
    loads[7].wait()

    loads[3].wait()
    keep_split(core)
    waiter(inverse.at[1 - core], inverse_sem).wait_recv()
    keep_split(1 - core)

    def select(a):
        for t in range(0, GROUP, 2):
            numbers = jnp.concatenate([ids[a * GROUP + t], ids[a * GROUP + t + 1]], axis=1)
            lane, block = numbers & (LANES - 1), numbers >> 7
            shape = (LANES, 2 * LANES)
            at_lane = lax.broadcasted_iota(jnp.int32, shape, 0) == jnp.broadcast_to(lane, shape)
            at_lane = jnp.where(at_lane, 1.0, 0.0).astype(jnp.bfloat16)
            picks = []
            for b in range(chips):
                at_block = jnp.where(block == b, 1.0, 0.0).astype(jnp.bfloat16)
                picks.append(at_lane * jnp.broadcast_to(at_block, shape))
            chosen = jnp.dot(
                halves[...], jnp.concatenate(picks, axis=0), preferred_element_type=jnp.float32
            )
            start = pl.multiple_of((a * GROUP + t) * LANES, 2 * LANES)
            selected[:, pl.ds(start, 2 * LANES)] = chosen.astype(jnp.bfloat16)

    near_to_far(ids, ids_sem, select)
    waiter(inverse_h, inverse_sem).wait_send()
    sent(ids, ids_sem)

    def faces_of(field):
        for b in range(blocks):
            by_block[b] = field[:, b * LANES : (b + 1) * LANES]
        return jnp.concatenate([by_block[faces_s[0, f]] for f in range(6)], axis=1)

    def sweep(k, carry):
        waiter(coarse.at[k, pl.ds(1, chips - 1)], coarse_sem.at[k]).wait_recv()
        gathered = jnp.concatenate([coarse[k, s] for s in range(chips)], axis=1)
        both = dot_nt(gathered, selected[...])
        both = both[:, : 2 * held] + both[:, 2 * held :]
        mine = both[0:rights] + both[rights:]
        partial[k, 0] = mine
        send(partial.at[k, 0], partial.at[k, 1], partial_sem.at[k], mate, j)
        base = u_ref[...] + weights[...] * r_ref[...]
        base_faces = faces_of(base)
        waiter(partial.at[k, 1], partial_sem.at[k]).wait_recv()
        solved[k, 0] = (mine + partial[k, 1]).astype(jnp.bfloat16)
        to_peers(solved.at[k], solved_sem.at[k])

        numbers = own_map[...]
        lane, chip = numbers & (LANES - 1), numbers >> 7
        slot = ((z + groups - (chip >> 2)) & 3) * GROUP + ((x + GROUP - (chip & 3)) & 3)
        waiter(solved.at[k, pl.ds(1, chips - 1)], solved_sem.at[k]).wait_recv()
        own = jnp.zeros((rights, LANES), jnp.float32)
        for s in range(chips):
            own = jnp.where(slot == s, lanes_of(solved[k, s].astype(jnp.float32), lane), own)
        own = own.astype(jnp.bfloat16)
        u_faces = (base_faces + dot(own, face_basis_t[...])).astype(jnp.bfloat16)
        for f in range(6):
            faces_out[k, f] = u_faces[:, f * LANES : (f + 1) * LANES]
        sems = face_sem.at[k]

        for f, by in ((1, 1), (0, regs - 1), (3, stride), (2, regs - stride)):
            send(faces_out.at[k, f], faces_in.at[k, f ^ 1], sems, i, (j + by) % regs)
        send(faces_out.at[k, 4], faces_in.at[k, 5], sems, before, j)
        send(faces_out.at[k, 5], faces_in.at[k, 4], sems, after, j)

        u = base + dot(own, basis_t[...])
        u_ref[...] = u
        result_o[0] = u.astype(result_o.dtype)
        here = rhs[...] - dot_nt(u.astype(jnp.bfloat16), dense[...])
        here_faces = faces_of(here)
        inside = [
            jnp.where(face_on[b] == 6, here[:, b * LANES : (b + 1) * LANES], 0.0) for b in range(blocks)
        ]
        coarse_inside = on_basis(jnp.concatenate(inside, axis=1))
        waiter(coarse.at[k, pl.ds(1, chips - 1)], coarse_sem.at[k]).wait_send()
        waiter(partial.at[k, 0], partial_sem.at[k]).wait_send()
        waiter(solved.at[k, pl.ds(1, chips - 1)], solved_sem.at[k]).wait_send()

        waiter(faces_in.at[k], sems).wait_recv()
        coupling = [0.5 * lanes_of(faces_in[k, f].astype(jnp.float32), match[f]) for f in range(6)]

        @pl.when(k < SWEEPS - 1)
        def _():
            r_faces = here_faces + jnp.concatenate(coupling, axis=1)
            keep_coarse(k + 1, coarse_inside + dot(r_faces.astype(jnp.bfloat16), face_basis[...]))
            to_peers(coarse.at[k + 1], coarse_sem.at[k + 1])

        for f in range(6):
            permuted[f] = coupling[f]
        r = here + jnp.concatenate([permuted[face_on[b]] for b in range(blocks)], axis=1)
        r_ref[...] = r
        result_o[1] = r.astype(result_o.dtype)
        return carry

    lax.fori_loop(0, SWEEPS, sweep, 0)

    for k in range(SWEEPS):
        waiter(faces_out.at[k], face_sem.at[k]).wait_send()


def body(
    right_side,
    tiles,
    tile_list,
    weights,
    face_map,
    matching,
    coarse_basis,
    coarse_map,
    coarse_inverse,
):
    _, _, order, rights = right_side.shape
    listed, tile = tiles.shape[2:4]
    held, coarse_all = coarse_inverse.shape[1:]
    n_coarse = coarse_map.shape[2]
    subs, regs = lax.axis_size("sub"), lax.axis_size("reg")
    chips = subs // 2
    blocks = order // tile
    f32, bf16, i32 = jnp.float32, jnp.bfloat16, jnp.int32
    vmem = pltpu.VMEM
    dma = pltpu.SemaphoreType.DMA
    hbm = pl.BlockSpec(memory_space=pltpu.HBM)
    result = pl.pallas_call(
        functools.partial(kernel, subs, regs),
        out_shape=pltpu.VMEM((2, rights, order), bf16),
        in_specs=[hbm] * 9,
        out_specs=pl.BlockSpec(memory_space=pltpu.VMEM),
        scratch_shapes=[
            vmem((rights, order), f32),
            vmem((listed + 1, tile, tile), bf16),
            vmem((2, listed), i32),
            vmem((1, order), f32),
            vmem((6, 1, tile), i32),
            vmem((blocks, tile, n_coarse), bf16),
            vmem((n_coarse, order), bf16),
            vmem((6 * tile, n_coarse), bf16),
            vmem((n_coarse, 6 * tile), bf16),
            pltpu.SMEM((1, 6), i32),
            vmem((1, n_coarse), i32),
            vmem((2, held, coarse_all), f32),
            vmem((4 * held, coarse_all), bf16),
            vmem((order, order), bf16),
            vmem((4 * held, chips * n_coarse), bf16),
            vmem((1, LANES), i32),
            pltpu.SMEM((1, LANES), i32),
            vmem((chips, 1, n_coarse), i32),
            vmem((SWEEPS, chips, 2 * rights, n_coarse), bf16),
            vmem((SWEEPS, 2, rights, 2 * held), f32),
            vmem((SWEEPS, chips, rights, 2 * held), bf16),
            vmem((blocks, rights, tile), f32),
            vmem((SWEEPS, 6, rights, tile), bf16),
            vmem((SWEEPS, 6, rights, tile), bf16),
            vmem((7, rights, tile), f32),
            vmem((rights, order), f32),
            vmem((rights, order), f32),
            dma((9,)),
            dma,
            dma((2,)),
            dma((GROUP, 2)),
            dma((SWEEPS, 2)),
            dma((SWEEPS, 2)),
            dma((SWEEPS, 2)),
            dma((SWEEPS, 2)),
        ],
        compiler_params=pltpu.CompilerParams(
            collective_id=0, has_side_effects=True, vmem_limit_bytes=56 * 2**20
        ),
        cost_estimate=pl.CostEstimate(
            flops=SWEEPS * 2 * rights * order * (order + 2 * n_coarse),
            bytes_accessed=listed * tile * tile * 2 + held * coarse_all * 8,
            transcendentals=0,
        ),
        name="richardson",
    )(
        right_side[0, 0].T,
        tiles[0, 0],
        tile_list[0, 0].T,
        weights[0],
        face_map[0],
        matching.reshape(6, 1, tile),
        coarse_basis.reshape(blocks, tile, n_coarse),
        coarse_map[0],
        coarse_inverse[0],
    )
    return tuple(result[n].T.reshape(1, 1, order, rights).astype(bf16) for n in range(2))


def solution(mesh):
    placed = (
        P("sub", "reg", None, None),
        P("sub", "reg", None, None, None),
        P("sub", "reg", None, None),
        P("sub", "reg", None),
        P("sub", "reg", None),
        P("sub", "reg", None, None),
        P("sub", "reg", None, None),
        P("sub", "reg", None),
        P("reg", "sub", None),
    )
    return jax.shard_map(
        body,
        mesh=mesh,
        in_specs=placed,
        out_specs=(P("sub", "reg", None, None), P("sub", "reg", None, None)),
        check_vma=False,
    )
```
